512 devices in a mesh: lat: 32 (over y, z_hi, x), lon: 16 (over z_lo, core).
Axes of the slice: x: 4, y: 4, z: 16 (z_hi: 2, z_lo: 8; z = z_hi * 8 + z_lo), core: 2. Of those that a mesh axis runs over, the one named last changes fastest.
Arguments:
- members: bfloat16 [40, 1024, 4096], P(None, 'lat', 'lon'), may hold values from -6 to 6
- support: int32 [1024], replicated, may hold values from 32 to 2048, as said below
Outputs:
- localized: float32 [40, 1024, 4096], P(None, 'lat', 'lon')
The draws below stay inside these ranges and needn't reach their ends.
Inputs may be any that keep to these rules, and one draw needn't show every extreme that they name: For rows r with 64 <= r < 960, support[r] <= 256; support[r] >= 32 everywhere.
All inputs are finite; a program needn't handle non-finite values.
Results may differ from the reference program's by a relative error of at most 0.0045.
Values may be sent and summed in bfloat16 or wider, within the bound.
No kernel may reach another device: no remote copies, remote signals or barrier semaphores. Data moves between devices by JAX's collectives and lax.ppermute only.
A program may use at most 64 MiB of HBM per device.

```python
import jax
import jax.numpy as jnp
from jax import lax

M = 40
NLON = 4096
HALF_LAT = 24
NLAT = 1024
LON_DEV = 256
POLAR = 64


def draw_support(key, part):
    key = jax.random.fold_in(key, 5)
    rows_all = jnp.arange(NLAT)
    from_pole = jnp.minimum(rows_all, NLAT - 1 - rows_all)
    equator_width = NLON // 128
    base_width = jnp.maximum(equator_width, equator_width * 14 * NLAT // (11 * (2 * from_pole + 1)))
    jitter = jax.random.randint(key, (NLAT,), 0, equator_width // 2 + 1) * (from_pole != NLAT // 2 - 1)
    widths = jnp.minimum(base_width + jitter, NLON // 2)
    polar_rows = (rows_all < POLAR) | (rows_all >= NLAT - POLAR)
    widths = jnp.where(polar_rows, widths, jnp.minimum(widths, LON_DEV))
    return jnp.maximum(widths, 1).astype(jnp.int32)


def block_levels(stream_key, dims, cuts, least, high):
    loudness = 1.0
    for axis_at, shards_of in cuts:
        heights = jax.random.uniform(jax.random.fold_in(jax.random.fold_in(stream_key, 6), axis_at), (shards_of,), jnp.float32, least / len(cuts), high / len(cuts))
        loudness = loudness * jnp.repeat(jnp.exp(heights), dims[axis_at] // shards_of).reshape((-1,) + (1,) * (len(dims) - 1 - axis_at))
    return loudness


def centred(own_key, dims, spread, most, pieces=(), dtype=jnp.bfloat16):
    result = jax.random.normal(own_key, dims, jnp.float32) * spread
    if len(pieces) > 0:
        result = block_levels(own_key, dims, pieces, -0.22, 0.18) * result
    return jnp.clip(result, min=-most, max=most).astype(dtype)


def setup_inputs(seed: int = 0) -> dict:
    seeds = jax.random.split(jax.random.key(seed), 3)
    return {
        "members": centred(seeds[0], (M, NLAT, NLON), 1.0, 6.0, ((1, 32), (2, 16))),
        "support": draw_support(jax.random.fold_in(seeds[2], 71), 0),
    }


def reference(members, support):
    cycle_cols = jnp.arange(NLON)
    distance = jnp.minimum(cycle_cols, NLON - cycle_cols).astype(jnp.float32)[None, :]
    width_f = support.astype(jnp.float32)[:, None]
    weights_raw = jnp.where(distance <= width_f, jnp.exp(-2.0 * distance * distance / (width_f * width_f)), 0.0)
    row_norms = 1.0 / jnp.sqrt(lax.optimization_barrier(jnp.sum(weights_raw * weights_raw, axis=1)))
    kernel = (weights_raw * row_norms[:, None]).astype(jnp.bfloat16)
    spectrum = jnp.fft.rfft(members.astype(jnp.float32), axis=2) * jnp.fft.rfft(kernel.astype(jnp.float32), axis=1)[None]
    along = jnp.fft.irfft(spectrum, n=NLON, axis=2).astype(jnp.float32).astype(jnp.bfloat16)
    padded = jnp.pad(along.astype(jnp.float32), ((0, 0), (HALF_LAT, HALF_LAT), (0, 0)))
    rows_all = jnp.arange(NLAT)
    total = jnp.zeros((M, NLAT, NLON), jnp.float32)
    squares = jnp.zeros((NLAT,), jnp.float32)
    for offset in range(-HALF_LAT, HALF_LAT + 1):
        value = jnp.exp(jnp.float32(-2.0 * offset * offset / (HALF_LAT * HALF_LAT)))
        weight_b = value.astype(jnp.bfloat16).astype(jnp.float32)
        total = total + weight_b * padded[:, HALF_LAT + offset:HALF_LAT + offset + NLAT, :]
        inside = (rows_all + offset >= 0) & (rows_all + offset < NLAT)
        squares = squares + jnp.where(inside, value * value, 0.0)
    lat_norms = 1.0 / jnp.sqrt(squares)
    return total * lat_norms[None, :, None]
```

```python
import functools

import jax
import jax.numpy as jnp
from jax import lax
from jax.experimental import pallas as pl
from jax.experimental.pallas import tpu as pltpu
from jax.sharding import PartitionSpec as P

HALF_LAT = 24
POLAR = 64
X_RUN = 4
TILE = 128


def flat_pairs(lat_count, lon_count, target):
    pairs = []
    for lat in range(lat_count):
        for lon in range(lon_count):
            to = target(lat, lon)
            if to is not None and 0 <= to[0] < lat_count:
                pairs.append((lat * lon_count + lon, to[0] * lon_count + to[1] % lon_count))
    return pairs


def toeplitz(offset, square, falloff, scale, nlon_all=None):
    distance = jnp.abs(offset)
    if nlon_all is not None:
        distance = jnp.minimum(distance, nlon_all - distance)
    distance_sq = distance * distance
    raw = jnp.where(distance_sq <= square, jnp.exp(distance_sq * falloff), 0.0)
    return (raw * scale).astype(jnp.bfloat16)


def near_kernel(width_ref, scale_ref, left_ref, mid_ref, right_ref, out_ref):
    rows = mid_ref.shape[0]
    first = pl.program_id(0) * rows
    base = (
        lax.broadcasted_iota(jnp.int32, (TILE, TILE), 0)
        - lax.broadcasted_iota(jnp.int32, (TILE, TILE), 1)
    ).astype(jnp.float32)
    zero = jnp.zeros((TILE, TILE), jnp.bfloat16)
    for row in range(rows):
        width = width_ref[first + row]
        scale = scale_ref[first + row]
        square = width * width
        falloff = -2.0 / square
        t = {3: zero, -3: zero}
        for k in range(-2, 3):
            t[k] = toeplitz(base + float(k * TILE), square, falloff, scale)
        weights = jnp.concatenate(
            [jnp.concatenate([t[a - 2], t[a - 3]], axis=1) for a in range(6)], axis=0
        )
        data = jnp.concatenate([left_ref[row], mid_ref[row], right_ref[row]], axis=1)
        out_ref[row] = jnp.dot(data, weights, preferred_element_type=jnp.float32).astype(
            jnp.bfloat16
        )


def near_product(left, mid, right, widths, scales):
    rows, members, cols = mid.shape
    step = 8
    block = pl.BlockSpec((step, members, cols), lambda i: (i, 0, 0))
    smem = pl.BlockSpec(memory_space=pltpu.SMEM)
    return pl.pallas_call(
        near_kernel,
        grid=(rows // step,),
        in_specs=[smem, smem, block, block, block],
        out_specs=block,
        out_shape=jax.ShapeDtypeStruct(mid.shape, jnp.bfloat16),
        compiler_params=pltpu.CompilerParams(vmem_limit_bytes=48 * 1024 * 1024),
    )(widths, scales, left, mid, right)


def circle_kernel(blocks, width_ref, scale_ref, data_ref, out_ref, twice, total):
    size, cols = data_ref.shape[1:]
    span = size // blocks
    nlon_all = float(blocks * cols)
    base = (
        lax.broadcasted_iota(jnp.int32, (cols, cols), 0)
        - lax.broadcasted_iota(jnp.int32, (cols, cols), 1)
    ).astype(jnp.float32)
    for row in range(data_ref.shape[0]):
        twice[:size] = data_ref[row]
        twice[size:] = data_ref[row]
        width = width_ref[row]
        scale = scale_ref[row]
        square = width * width
        falloff = -2.0 / square
        total[...] = jnp.zeros_like(total)

        def step(k, carry):
            offset = base + (k * cols).astype(jnp.float32)
            weights = toeplitz(offset, square, falloff, scale, nlon_all)
            data = twice[pl.ds(pl.multiple_of(k * span, 16), size)]
            total[...] += jnp.dot(data, weights, preferred_element_type=jnp.float32)
            return carry

        lax.fori_loop(0, blocks, step, 0)
        out_ref[row] = total[...].astype(jnp.bfloat16)


def circle_product(data, widths, scales, blocks):
    rows, size, cols = data.shape
    smem = pl.BlockSpec(memory_space=pltpu.SMEM)
    vmem = pl.BlockSpec(memory_space=pltpu.VMEM)
    return pl.pallas_call(
        functools.partial(circle_kernel, blocks),
        in_specs=[smem, smem, vmem],
        out_specs=vmem,
        out_shape=jax.ShapeDtypeStruct(data.shape, jnp.bfloat16),
        scratch_shapes=[
            pltpu.VMEM((2 * size, cols), jnp.bfloat16),
            pltpu.VMEM((size, cols), jnp.float32),
        ],
        compiler_params=pltpu.CompilerParams(vmem_limit_bytes=48 * 1024 * 1024),
    )(widths, scales, data)


def row_scale(width_f, nlon_all):
    cycle_cols = jnp.arange(nlon_all)
    distance = jnp.minimum(cycle_cols, nlon_all - cycle_cols).astype(jnp.float32)[None, :]
    width_f = width_f[:, None]
    weights_raw = jnp.where(
        distance <= width_f, jnp.exp(-2.0 * distance * distance / (width_f * width_f)), 0.0
    )
    return 1.0 / jnp.sqrt(jnp.sum(weights_raw * weights_raw, axis=1))


def polar_along(data, widths, scales):
    rows, members, cols = data.shape
    lon_count = lax.axis_size("lon")
    own = rows // lon_count
    padded = -members % 16
    parts = data.reshape(lon_count, own, members, cols)
    parts = lax.all_to_all(parts, "lon", 0, 0)
    parts = jnp.pad(parts.transpose(1, 0, 2, 3), ((0, 0), (0, 0), (0, padded), (0, 0)))
    parts = parts.reshape(own, lon_count * (members + padded), cols)
    first = lax.axis_index("lon") * own
    result = circle_product(
        parts,
        lax.dynamic_slice_in_dim(widths, first, own),
        lax.dynamic_slice_in_dim(scales, first, own),
        lon_count,
    )
    result = result.reshape(own, lon_count, members + padded, cols)[:, :, :members]
    result = lax.all_to_all(result.transpose(1, 0, 2, 3), "lon", 0, 0)
    return result.reshape(rows, members, cols)


def lat_halo(along, lat_index, lat_count, lon_count):
    axes = ("lat", "lon")
    last, x = X_RUN - 1, lat_index % X_RUN
    pairs = functools.partial(flat_pairs, lat_count, lon_count)
    lower, upper = along[:HALF_LAT], along[-HALF_LAT:]
    far = lax.ppermute(
        jnp.where(x == last, upper, lower),
        axes,
        pairs(
            lambda lat, lon: (lat + 1, lon)
            if lat % X_RUN == last
            else ((lat - 1, lon) if lat % X_RUN == 0 else None)
        ),
    )
    low = lax.ppermute(
        upper, axes, pairs(lambda lat, lon: (lat + 1, lon) if lat % X_RUN != last else None)
    )
    high = lax.ppermute(
        lower, axes, pairs(lambda lat, lon: (lat - 1, lon) if lat % X_RUN != 0 else None)
    )
    return jnp.where(x == 0, far, low), jnp.where(x == last, far, high)


def body(members, support):
    member_count, lat_rows, lon_cols = members.shape
    lat_count = lax.axis_size("lat")
    lon_count = lax.axis_size("lon")
    nlon_all = lon_count * lon_cols
    nlat_all = lat_count * lat_rows
    lat_index = lax.axis_index("lat")
    axes = ("lat", "lon")

    def polar_of(lat):
        return (lat * lat_rows < POLAR) | ((lat + 1) * lat_rows > nlat_all - POLAR)

    pairs = functools.partial(flat_pairs, lat_count, lon_count)
    data = members.transpose(1, 0, 2)
    left = lax.ppermute(
        data, axes, pairs(lambda lat, lon: None if polar_of(lat) else (lat, lon + 1))
    )
    right = lax.ppermute(
        data, axes, pairs(lambda lat, lon: None if polar_of(lat) else (lat, lon - 1))
    )
    widths = lax.dynamic_slice_in_dim(support, lat_index * lat_rows, lat_rows).astype(jnp.float32)
    scales = row_scale(widths, nlon_all)
    along = lax.cond(
        polar_of(lat_index),
        lambda: polar_along(data, widths, scales),
        lambda: near_product(left, data, right, widths, scales),
    )

    low, high = lat_halo(along, lat_index, lat_count, lon_count)
    widened = jnp.concatenate([low, along, high], axis=0)

    half_rows = HALF_LAT
    source_rows = jnp.arange(lat_rows + 2 * half_rows)
    own_rows = jnp.arange(lat_rows)
    offsets_band = (source_rows[:, None] - half_rows - own_rows[None, :]).astype(jnp.float32)
    banded = jnp.where(
        jnp.abs(offsets_band) <= half_rows,
        jnp.exp(-2.0 * offsets_band * offsets_band / (half_rows * half_rows)),
        0.0,
    ).astype(jnp.bfloat16)
    global_rows = lat_index * lat_rows + own_rows
    offsets = jnp.arange(-half_rows, half_rows + 1)
    offset_f = offsets.astype(jnp.float32)
    values = jnp.exp(-2.0 * offset_f * offset_f / (half_rows * half_rows))
    reached = global_rows[:, None] + offsets[None, :]
    inside = (reached >= 0) & (reached < nlat_all)
    lat_norms = 1.0 / jnp.sqrt(jnp.sum(jnp.where(inside, (values * values)[None, :], 0.0), axis=1))
    smoothed = jnp.einsum("jmc,jr->mrc", widened, banded, preferred_element_type=jnp.float32)
    return smoothed * lat_norms[None, :, None]


def solution(mesh):
    placed = (P(None, "lat", "lon"), P())
    return jax.shard_map(
        body, mesh=mesh, in_specs=placed, out_specs=P(None, "lat", "lon"), check_vma=False
    )
```

```python
import functools

import jax
import jax.numpy as jnp
from jax import lax
from jax.experimental import pallas as pl
from jax.experimental.pallas import tpu as pltpu
from jax.sharding import PartitionSpec as P

HALF_LAT = 24
POLAR = 64
X_RUN = 4
HELPERS = {0: (10, 26, 17, 18), 1: (1, 9, 25, 2), 30: (30, 22, 6, 29), 31: (21, 5, 14, 13)}
TILE = 128


def flat_pairs(lat_count, lon_count, target):
    pairs = []
    for lat in range(lat_count):
        for lon in range(lon_count):
            to = target(lat, lon)
            if to is not None and 0 <= to[0] < lat_count:
                pairs.append((lat * lon_count + lon, to[0] * lon_count + to[1] % lon_count))
    return pairs


def toeplitz(offset, square, falloff, scale, nlon_all=None):
    distance = jnp.abs(offset)
    if nlon_all is not None:
        distance = jnp.minimum(distance, nlon_all - distance)
    distance_sq = distance * distance
    raw = jnp.where(distance_sq <= square, jnp.exp(distance_sq * falloff), 0.0)
    return (raw * scale).astype(jnp.bfloat16)


def near_kernel(width_ref, scale_ref, left_ref, mid_ref, right_ref, out_ref):
    rows = mid_ref.shape[0]
    first = pl.program_id(0) * rows
    base = (
        lax.broadcasted_iota(jnp.int32, (TILE, TILE), 0)
        - lax.broadcasted_iota(jnp.int32, (TILE, TILE), 1)
    ).astype(jnp.float32)
    zero = jnp.zeros((TILE, TILE), jnp.bfloat16)
    for row in range(rows):
        width = width_ref[first + row]
        scale = scale_ref[first + row]
        square = width * width
        falloff = -2.0 / square
        t = {3: zero, -3: zero}
        for k in range(-2, 3):
            t[k] = toeplitz(base + float(k * TILE), square, falloff, scale)
        weights = jnp.concatenate(
            [jnp.concatenate([t[a - 2], t[a - 3]], axis=1) for a in range(6)], axis=0
        )
        data = jnp.concatenate([left_ref[row], mid_ref[row], right_ref[row]], axis=1)
        out_ref[row] = jnp.dot(data, weights, preferred_element_type=jnp.float32).astype(
            jnp.bfloat16
        )


def near_product(left, mid, right, widths, scales):
    rows, members, cols = mid.shape
    step = 8
    block = pl.BlockSpec((step, members, cols), lambda i: (i, 0, 0))
    smem = pl.BlockSpec(memory_space=pltpu.SMEM)
    return pl.pallas_call(
        near_kernel,
        grid=(rows // step,),
        in_specs=[smem, smem, block, block, block],
        out_specs=block,
        out_shape=jax.ShapeDtypeStruct(mid.shape, jnp.bfloat16),
        compiler_params=pltpu.CompilerParams(vmem_limit_bytes=48 * 1024 * 1024),
    )(widths, scales, left, mid, right)


def circle_kernel(blocks, width_ref, scale_ref, data_ref, out_ref, twice, total):
    size, cols = data_ref.shape[1:]
    span = size // blocks
    nlon_all = float(blocks * cols)
    base = (
        lax.broadcasted_iota(jnp.int32, (cols, cols), 0)
        - lax.broadcasted_iota(jnp.int32, (cols, cols), 1)
    ).astype(jnp.float32)
    for row in range(data_ref.shape[0]):
        twice[:size] = data_ref[row]
        twice[size:] = data_ref[row]
        width = width_ref[row]
        scale = scale_ref[row]
        square = width * width
        falloff = -2.0 / square
        total[...] = jnp.zeros_like(total)

        def step(k, carry):
            offset = base + (k * cols).astype(jnp.float32)
            weights = toeplitz(offset, square, falloff, scale, nlon_all)
            data = twice[pl.ds(pl.multiple_of(k * span, 16), size)]
            total[...] += jnp.dot(data, weights, preferred_element_type=jnp.float32)
            return carry

        lax.fori_loop(0, blocks, step, 0, unroll=4)
        out_ref[row] = total[...].astype(jnp.bfloat16)


def circle_product(data, widths, scales, blocks):
    rows, size, cols = data.shape
    smem = pl.BlockSpec(memory_space=pltpu.SMEM)
    vmem = pl.BlockSpec(memory_space=pltpu.VMEM)
    return pl.pallas_call(
        functools.partial(circle_kernel, blocks),
        in_specs=[smem, smem, vmem],
        out_specs=vmem,
        out_shape=jax.ShapeDtypeStruct(data.shape, jnp.bfloat16),
        scratch_shapes=[
            pltpu.VMEM((2 * size, cols), jnp.bfloat16),
            pltpu.VMEM((size, cols), jnp.float32),
        ],
        compiler_params=pltpu.CompilerParams(vmem_limit_bytes=48 * 1024 * 1024),
    )(widths, scales, data)


def row_scale(width_f, nlon_all):
    cycle_cols = jnp.arange(nlon_all)
    distance = jnp.minimum(cycle_cols, nlon_all - cycle_cols).astype(jnp.float32)[None, :]
    width_f = width_f[:, None]
    weights_raw = jnp.where(
        distance <= width_f, jnp.exp(-2.0 * distance * distance / (width_f * width_f)), 0.0
    )
    return 1.0 / jnp.sqrt(jnp.sum(weights_raw * weights_raw, axis=1))


def unit_product(parts, width, scale):
    blocks, members, cols = parts.shape
    padded = members + -members % 16
    data = jnp.pad(parts, ((0, 0), (0, padded - members), (0, 0)))
    result = circle_product(data.reshape(1, blocks * padded, cols), width, scale, blocks)
    return result.reshape(blocks, padded, cols)[:, :members]


def far_halo(near, lat_index, lat_count, lon_count):
    last = X_RUN - 1
    send = jnp.where(lat_index % X_RUN == last, near[-HALF_LAT:], near[:HALF_LAT])

    def across(lat, lon):
        return {last: (lat + 1, lon), 0: (lat - 1, lon)}.get(lat % X_RUN)

    return lax.ppermute(send, ("lat", "lon"), flat_pairs(lat_count, lon_count, across))


def next_halo(along, lat_count, lon_count):
    axes = ("lat", "lon")
    last = X_RUN - 1
    pairs = functools.partial(flat_pairs, lat_count, lon_count)
    low = lax.ppermute(
        along[-HALF_LAT:],
        axes,
        pairs(lambda lat, lon: (lat + 1, lon) if lat % X_RUN != last else None),
    )
    high = lax.ppermute(
        along[:HALF_LAT],
        axes,
        pairs(lambda lat, lon: (lat - 1, lon) if lat % X_RUN != 0 else None),
    )
    return low, high


def body(members, support):
    member_count, lat_rows, lon_cols = members.shape
    lat_count = lax.axis_size("lat")
    lon_count = lax.axis_size("lon")
    nlon_all = lon_count * lon_cols
    nlat_all = lat_count * lat_rows
    lat_index = lax.axis_index("lat")
    axes = ("lat", "lon")

    def polar_of(lat):
        return (lat * lat_rows < POLAR) | ((lat + 1) * lat_rows > nlat_all - POLAR)

    pairs = functools.partial(flat_pairs, lat_count, lon_count)
    data = members.transpose(1, 0, 2)
    lon_index = lax.axis_index("lon")

    shares = len(HELPERS[0])
    share = lat_rows // shares
    helped = {h: (p, q) for p, hs in HELPERS.items() for q, h in enumerate(hs)}
    pieces = lon_count // share
    is_polar = polar_of(lat_index)
    takes_part = functools.reduce(lambda a, b: a | b, [lat_index == i for i in helped])
    keeps = functools.reduce(lambda a, b: a | b, [lat_index == p for p in HELPERS if p in helped])
    row_of = jnp.array(
        [helped[i][0] * lat_rows + helped[i][1] * share if i in helped else 0 for i in range(lat_count)]
    )[lat_index]

    def hands(q):
        return lambda lat, lon: (
            (HELPERS[lat][q], lon) if lat in HELPERS and HELPERS[lat][q] != lat else None
        )

    def returns(q):
        return lambda lat, lon: (
            (helped[lat][0], lon) if lat in helped and helped[lat][1] == q and helped[lat][0] != lat else None
        )

    handed = [
        lax.ppermute(data[q * share : (q + 1) * share], axes, pairs(hands(q))) for q in range(shares)
    ]
    given = jnp.where(keeps, data[:share], sum(handed))
    parts = given.reshape(lon_count, member_count // pieces, lon_cols)

    left = lax.ppermute(
        data, axes, pairs(lambda lat, lon: None if polar_of(lat) else (lat, lon + 1))
    )
    right = lax.ppermute(
        data, axes, pairs(lambda lat, lon: None if polar_of(lat) else (lat, lon - 1))
    )
    widths = lax.dynamic_slice_in_dim(support, lat_index * lat_rows, lat_rows).astype(jnp.float32)
    unit_width = lax.dynamic_slice_in_dim(support, row_of + lon_index // pieces, 1).astype(jnp.float32)
    scales = row_scale(jnp.concatenate([widths, unit_width]), nlon_all)
    scales, unit_scale = scales[:lat_rows], scales[lat_rows:]

    def helping(parts):
        parts = lax.all_to_all(parts, "lon", 0, 0)
        return lax.all_to_all(unit_product(parts, unit_width, unit_scale), "lon", 0, 0)

    parts = lax.cond(takes_part, helping, lambda v: v, parts)
    parts, left, right = lax.optimization_barrier((parts, left, right))
    near = near_product(left, data, right, widths, scales)

    far = far_halo(near, lat_index, lat_count, lon_count)
    done = parts.reshape(share, member_count, lon_cols)
    polar = [lax.ppermute(done, axes, pairs(returns(q))) for q in range(shares)]
    polar[0] = jnp.where(keeps, done, polar[0])
    polar = jnp.concatenate(polar, axis=0)
    along = jnp.where(is_polar, polar, near)
    low, high = next_halo(along, lat_count, lon_count)

    half_rows = HALF_LAT
    source_rows = jnp.arange(lat_rows + 2 * half_rows)
    own_rows = jnp.arange(lat_rows)
    offsets_band = (source_rows[:, None] - half_rows - own_rows[None, :]).astype(jnp.float32)
    banded = jnp.where(
        jnp.abs(offsets_band) <= half_rows,
        jnp.exp(-2.0 * offsets_band * offsets_band / (half_rows * half_rows)),
        0.0,
    ).astype(jnp.bfloat16)
    global_rows = lat_index * lat_rows + own_rows
    offsets = jnp.arange(-half_rows, half_rows + 1)
    offset_f = offsets.astype(jnp.float32)
    values = jnp.exp(-2.0 * offset_f * offset_f / (half_rows * half_rows))
    reached = global_rows[:, None] + offsets[None, :]
    inside = (reached >= 0) & (reached < nlat_all)
    lat_norms = 1.0 / jnp.sqrt(jnp.sum(jnp.where(inside, (values * values)[None, :], 0.0), axis=1))
    lower, own, upper = banded[:half_rows], banded[half_rows:-half_rows], banded[-half_rows:]
    x = lat_index % X_RUN
    taps = jnp.where(x == 0, lower, upper)
    first = jnp.einsum(
        "jmc,jr->mrc",
        jnp.concatenate([far, along], axis=0),
        jnp.concatenate([taps, own], axis=0),
        preferred_element_type=jnp.float32,
    )
    first = lax.optimization_barrier(first)
    second = jnp.einsum(
        "jmc,jr->mrc",
        jnp.concatenate([low, high], axis=0),
        jnp.concatenate([lower, upper], axis=0),
        preferred_element_type=jnp.float32,
    )
    return (first + second) * lat_norms[None, :, None]


def solution(mesh):
    placed = (P(None, "lat", "lon"), P())
    return jax.shard_map(
        body, mesh=mesh, in_specs=placed, out_specs=P(None, "lat", "lon"), check_vma=False
    )
```

```python
import functools

import jax
import jax.numpy as jnp
from jax import lax
from jax.experimental import pallas as pl
from jax.experimental.pallas import tpu as pltpu
from jax.sharding import PartitionSpec as P

HALF_LAT = 24
POLAR = 64
X_RUN = 4
HELPERS = {0: (2, 10, 26, 18), 1: (1, 9, 25, 17), 30: (30, 22, 6, 14), 31: (29, 21, 5, 13)}
TILE = 128


def flat_pairs(lat_count, lon_count, target):
    pairs = []
    for lat in range(lat_count):
        for lon in range(lon_count):
            to = target(lat, lon)
            if to is not None and 0 <= to[0] < lat_count:
                pairs.append((lat * lon_count + lon, to[0] * lon_count + to[1] % lon_count))
    return pairs


def toeplitz(offset, square, falloff, scale, nlon_all=None):
    distance = jnp.abs(offset)
    if nlon_all is not None:
        distance = jnp.minimum(distance, nlon_all - distance)
    distance_sq = distance * distance
    raw = jnp.where(distance_sq <= square, jnp.exp(distance_sq * falloff), 0.0)
    return (raw * scale).astype(jnp.bfloat16)


def near_kernel(width_ref, scale_ref, left_ref, mid_ref, right_ref, out_ref):
    rows = mid_ref.shape[0]
    first = pl.program_id(0) * rows
    base = (
        lax.broadcasted_iota(jnp.int32, (TILE, TILE), 0)
        - lax.broadcasted_iota(jnp.int32, (TILE, TILE), 1)
    ).astype(jnp.float32)
    zero = jnp.zeros((TILE, TILE), jnp.bfloat16)
    for row in range(rows):
        width = width_ref[first + row]
        scale = scale_ref[first + row]
        square = width * width
        falloff = -2.0 / square
        t = {3: zero, -3: zero}
        for k in range(-2, 3):
            t[k] = toeplitz(base + float(k * TILE), square, falloff, scale)
        weights = jnp.concatenate(
            [jnp.concatenate([t[a - 2], t[a - 3]], axis=1) for a in range(6)], axis=0
        )
        data = jnp.concatenate([left_ref[row], mid_ref[row], right_ref[row]], axis=1)
        out_ref[row] = jnp.dot(data, weights, preferred_element_type=jnp.float32).astype(
            jnp.bfloat16
        )


def near_product(left, mid, right, widths, scales):
    rows, members, cols = mid.shape
    step = 8
    block = pl.BlockSpec((step, members, cols), lambda i: (i, 0, 0))
    smem = pl.BlockSpec(memory_space=pltpu.SMEM)
    return pl.pallas_call(
        near_kernel,
        grid=(rows // step,),
        in_specs=[smem, smem, block, block, block],
        out_specs=block,
        out_shape=jax.ShapeDtypeStruct(mid.shape, jnp.bfloat16),
        compiler_params=pltpu.CompilerParams(vmem_limit_bytes=48 * 1024 * 1024),
    )(widths, scales, left, mid, right)


def circle_kernel(blocks, width_ref, scale_ref, data_ref, out_ref, twice, total):
    size, cols = data_ref.shape[1:]
    span = size // blocks
    nlon_all = float(blocks * cols)
    base = (
        lax.broadcasted_iota(jnp.int32, (cols, cols), 0)
        - lax.broadcasted_iota(jnp.int32, (cols, cols), 1)
    ).astype(jnp.float32)
    for row in range(data_ref.shape[0]):
        twice[:size] = data_ref[row]
        twice[size:] = data_ref[row]
        width = width_ref[row]
        scale = scale_ref[row]
        square = width * width
        falloff = -2.0 / square
        total[...] = jnp.zeros_like(total)

        def step(k, carry):
            offset = base + (k * cols).astype(jnp.float32)
            weights = toeplitz(offset, square, falloff, scale, nlon_all)
            data = twice[pl.ds(pl.multiple_of(k * span, 16), size)]
            total[...] += jnp.dot(data, weights, preferred_element_type=jnp.float32)
            return carry

        lax.fori_loop(0, blocks, step, 0, unroll=4)
        out_ref[row] = total[...].astype(jnp.bfloat16)


def circle_product(data, widths, scales, blocks):
    rows, size, cols = data.shape
    smem = pl.BlockSpec(memory_space=pltpu.SMEM)
    vmem = pl.BlockSpec(memory_space=pltpu.VMEM)
    return pl.pallas_call(
        functools.partial(circle_kernel, blocks),
        in_specs=[smem, smem, vmem],
        out_specs=vmem,
        out_shape=jax.ShapeDtypeStruct(data.shape, jnp.bfloat16),
        scratch_shapes=[
            pltpu.VMEM((2 * size, cols), jnp.bfloat16),
            pltpu.VMEM((size, cols), jnp.float32),
        ],
        compiler_params=pltpu.CompilerParams(vmem_limit_bytes=48 * 1024 * 1024),
    )(widths, scales, data)


def row_scale(width_f, nlon_all):
    cycle_cols = jnp.arange(nlon_all)
    distance = jnp.minimum(cycle_cols, nlon_all - cycle_cols).astype(jnp.float32)[None, :]
    width_f = width_f[:, None]
    weights_raw = jnp.where(
        distance <= width_f, jnp.exp(-2.0 * distance * distance / (width_f * width_f)), 0.0
    )
    return 1.0 / jnp.sqrt(jnp.sum(weights_raw * weights_raw, axis=1))


def unit_product(parts, width, scale):
    blocks, members, cols = parts.shape
    padded = members + -members % 16
    data = jnp.pad(parts, ((0, 0), (0, padded - members), (0, 0)))
    result = circle_product(data.reshape(1, blocks * padded, cols), width, scale, blocks)
    return result.reshape(blocks, padded, cols)[:, :members]


def far_halo(near, lat_index, lat_count, lon_count):
    last = X_RUN - 1
    send = jnp.where(lat_index % X_RUN == last, near[-HALF_LAT:], near[:HALF_LAT])

    def across(lat, lon):
        return {last: (lat + 1, lon), 0: (lat - 1, lon)}.get(lat % X_RUN)

    return lax.ppermute(send, ("lat", "lon"), flat_pairs(lat_count, lon_count, across))


def next_halo(along, lat_count, lon_count):
    axes = ("lat", "lon")
    last = X_RUN - 1
    pairs = functools.partial(flat_pairs, lat_count, lon_count)
    low = lax.ppermute(
        along[-HALF_LAT:],
        axes,
        pairs(lambda lat, lon: (lat + 1, lon) if lat % X_RUN != last else None),
    )
    high = lax.ppermute(
        along[:HALF_LAT],
        axes,
        pairs(lambda lat, lon: (lat - 1, lon) if lat % X_RUN != 0 else None),
    )
    return low, high


def body(members, support):
    member_count, lat_rows, lon_cols = members.shape
    lat_count = lax.axis_size("lat")
    lon_count = lax.axis_size("lon")
    nlon_all = lon_count * lon_cols
    nlat_all = lat_count * lat_rows
    lat_index = lax.axis_index("lat")
    axes = ("lat", "lon")

    def polar_of(lat):
        return (lat * lat_rows < POLAR) | ((lat + 1) * lat_rows > nlat_all - POLAR)

    pairs = functools.partial(flat_pairs, lat_count, lon_count)
    data = members.transpose(1, 0, 2)
    lon_index = lax.axis_index("lon")

    shares = len(HELPERS[0])
    share = lat_rows // shares
    helped = {h: (p, q) for p, hs in HELPERS.items() for q, h in enumerate(hs)}
    pieces = lon_count // share
    is_polar = polar_of(lat_index)
    takes_part = functools.reduce(lambda a, b: a | b, [lat_index == i for i in helped])
    keeps = functools.reduce(lambda a, b: a | b, [lat_index == p for p in HELPERS if p in helped])
    row_of = jnp.array(
        [helped[i][0] * lat_rows + helped[i][1] * share if i in helped else 0 for i in range(lat_count)]
    )[lat_index]

    def hands(q):
        return lambda lat, lon: (
            (HELPERS[lat][q], lon) if lat in HELPERS and HELPERS[lat][q] != lat else None
        )

    def returns(q):
        return lambda lat, lon: (
            (helped[lat][0], lon) if lat in helped and helped[lat][1] == q and helped[lat][0] != lat else None
        )

    handed = [
        lax.ppermute(data[q * share : (q + 1) * share], axes, pairs(hands(q))) for q in range(shares)
    ]
    handed[1], late = lax.optimization_barrier((handed[1], data))
    given = jnp.where(keeps, data[:share], sum(handed))
    parts = given.reshape(lon_count, member_count // pieces, lon_cols)

    left = lax.ppermute(
        data, axes, pairs(lambda lat, lon: None if polar_of(lat) else (lat, lon + 1))
    )
    right = lax.ppermute(
        late, axes, pairs(lambda lat, lon: None if polar_of(lat) else (lat, lon - 1))
    )
    widths = lax.dynamic_slice_in_dim(support, lat_index * lat_rows, lat_rows).astype(jnp.float32)
    unit_width = lax.dynamic_slice_in_dim(support, row_of + lon_index // pieces, 1).astype(jnp.float32)
    scales = row_scale(jnp.concatenate([widths, unit_width]), nlon_all)
    scales, unit_scale = scales[:lat_rows], scales[lat_rows:]

    def helping(parts):
        parts = lax.all_to_all(parts, "lon", 0, 0)
        return lax.all_to_all(unit_product(parts, unit_width, unit_scale), "lon", 0, 0)

    parts = lax.cond(takes_part, helping, lambda v: v, parts)
    parts, left, right = lax.optimization_barrier((parts, left, right))
    near = near_product(left, data, right, widths, scales)

    far = far_halo(near, lat_index, lat_count, lon_count)
    done = parts.reshape(share, member_count, lon_cols)
    polar = [lax.ppermute(done, axes, pairs(returns(q))) for q in range(shares)]
    polar[0] = jnp.where(keeps, done, polar[0])
    polar = jnp.concatenate(polar, axis=0)
    along = jnp.where(is_polar, polar, near)
    low, high = next_halo(along, lat_count, lon_count)

    half_rows = HALF_LAT
    source_rows = jnp.arange(lat_rows + 2 * half_rows)
    own_rows = jnp.arange(lat_rows)
    offsets_band = (source_rows[:, None] - half_rows - own_rows[None, :]).astype(jnp.float32)
    banded = jnp.where(
        jnp.abs(offsets_band) <= half_rows,
        jnp.exp(-2.0 * offsets_band * offsets_band / (half_rows * half_rows)),
        0.0,
    ).astype(jnp.bfloat16)
    global_rows = lat_index * lat_rows + own_rows
    offsets = jnp.arange(-half_rows, half_rows + 1)
    offset_f = offsets.astype(jnp.float32)
    values = jnp.exp(-2.0 * offset_f * offset_f / (half_rows * half_rows))
    reached = global_rows[:, None] + offsets[None, :]
    inside = (reached >= 0) & (reached < nlat_all)
    lat_norms = 1.0 / jnp.sqrt(jnp.sum(jnp.where(inside, (values * values)[None, :], 0.0), axis=1))
    lower, own, upper = banded[:half_rows], banded[half_rows:-half_rows], banded[-half_rows:]
    x = lat_index % X_RUN
    taps = jnp.where(x == 0, lower, upper)
    first = jnp.einsum(
        "jmc,jr->mrc",
        jnp.concatenate([far, along], axis=0),
        jnp.concatenate([taps, own], axis=0),
        preferred_element_type=jnp.float32,
    )
    first = lax.optimization_barrier(first)
    second = jnp.einsum(
        "jmc,jr->mrc",
        jnp.concatenate([low, high], axis=0),
        jnp.concatenate([lower, upper], axis=0),
        preferred_element_type=jnp.float32,
    )
    return (first + second) * lat_norms[None, :, None]


def solution(mesh):
    placed = (P(None, "lat", "lon"), P())
    return jax.shard_map(
        body, mesh=mesh, in_specs=placed, out_specs=P(None, "lat", "lon"), check_vma=False
    )
```

```python
import functools
import math

import jax
import jax.numpy as jnp
from jax import lax
from jax.experimental import pallas as pl
from jax.experimental.pallas import tpu as pltpu
from jax.sharding import PartitionSpec as P

HALF_LAT = 24
POLAR = 64
X_RUN = 4
HELPERS = {0: (2, 10, 26, 18), 1: (1, 9, 25, 17), 30: (30, 22, 6, 14), 31: (29, 21, 5, 13)}
TILE = 128
LOG2E = math.log2(math.e)


def flat_pairs(lat_count, lon_count, target):
    pairs = []
    for lat in range(lat_count):
        for lon in range(lon_count):
            to = target(lat, lon)
            if to is not None and 0 <= to[0] < lat_count:
                pairs.append((lat * lon_count + lon, to[0] * lon_count + to[1] % lon_count))
    return pairs


def difference(shape):
    return (lax.broadcasted_iota(jnp.int32, shape, 0) - lax.broadcasted_iota(jnp.int32, shape, 1)).astype(jnp.float32)

def toeplitz(distance_sq, square, falloff, level):
    value = jnp.exp2(distance_sq * falloff + level)
    return jnp.where(distance_sq <= square, value, 0.0).astype(jnp.bfloat16)


def near_kernel(width_ref, level_ref, left_ref, mid_ref, right_ref, out_ref):
    rows = mid_ref.shape[0]
    first = pl.program_id(0) * rows
    base = difference((TILE, TILE))
    distances = {k: (base + float(k * TILE)) * (base + float(k * TILE)) for k in range(-2, 3)}
    for row in range(rows):
        width = width_ref[first + row]
        level = level_ref[first + row]
        square = width * width
        falloff = (-2.0 * LOG2E) / square
        t = {}
        for k in range(-2, 3):
            t[k] = toeplitz(distances[k], square, falloff, level)
        weights = jnp.concatenate([t[k] for k in range(-2, 3)], axis=0)
        data = jnp.concatenate([left_ref[row], mid_ref[row], right_ref[row]], axis=1)
        both = jnp.concatenate([data[:, : 5 * TILE], data[:, TILE:]], axis=0)
        got = jnp.dot(both, weights, preferred_element_type=jnp.float32).astype(jnp.bfloat16)
        half = data.shape[0]
        out_ref[row] = jnp.concatenate([got[:half], got[half:]], axis=1)


def near_product(left, mid, right, widths, levels):
    rows, members, cols = mid.shape
    step = 16
    block = pl.BlockSpec((step, members, cols), lambda i: (i, 0, 0))
    smem = pl.BlockSpec(memory_space=pltpu.SMEM)
    return pl.pallas_call(
        near_kernel,
        grid=(rows // step,),
        in_specs=[smem, smem, block, block, block],
        out_specs=block,
        out_shape=jax.ShapeDtypeStruct(mid.shape, jnp.bfloat16),
        compiler_params=pltpu.CompilerParams(vmem_limit_bytes=48 * 1024 * 1024),
    )(widths, levels, left, mid, right)


def circle_kernel(width_ref, level_ref, data_ref, out_ref, tiles, twice, total):
    blocks, members, cols = data_ref.shape
    span = twice.shape[0] // (2 * blocks)
    size = blocks * span
    count = blocks * cols // TILE
    base = difference((TILE, TILE))
    width = width_ref[0]
    level = level_ref[0]
    square = width * width
    falloff = (-2.0 * LOG2E) / square
    for n in range(count // 2 + 1):
        distance = jnp.abs(base + float(n * TILE))
        distance = jnp.minimum(distance, float(count * TILE) - distance)
        tile = toeplitz(distance * distance, square, falloff, level)
        tiles[n] = tile
        if 0 < n < count // 2:
            tiles[count - n] = tile.T
    pad = jnp.zeros((span - members, cols), jnp.bfloat16)
    for i in range(blocks):
        block = jnp.concatenate([data_ref[i], pad], axis=0)
        twice[i * span : (i + 1) * span] = block
        twice[size + i * span : size + (i + 1) * span] = block
    for k in range(blocks):
        weights = jnp.concatenate(
            [
                jnp.concatenate([tiles[2 * k], tiles[(2 * k - 1) % count]], axis=1),
                jnp.concatenate([tiles[(2 * k + 1) % count], tiles[2 * k]], axis=1),
            ],
            axis=0,
        )
        part = jnp.dot(twice[k * span : k * span + size], weights, preferred_element_type=jnp.float32)
        if k == 0:
            total[...] = part
        else:
            total[...] += part
    for i in range(blocks):
        out_ref[i] = total[i * span : i * span + members].astype(jnp.bfloat16)


def unit_product(parts, width, level):
    blocks, members, cols = parts.shape
    span = members + -members % 16
    smem = pl.BlockSpec(memory_space=pltpu.SMEM)
    vmem = pl.BlockSpec(memory_space=pltpu.VMEM)
    return pl.pallas_call(
        circle_kernel,
        in_specs=[smem, smem, vmem],
        out_specs=vmem,
        out_shape=jax.ShapeDtypeStruct(parts.shape, jnp.bfloat16),
        scratch_shapes=[
            pltpu.VMEM((blocks * cols // TILE, TILE, TILE), jnp.bfloat16),
            pltpu.VMEM((2 * blocks * span, cols), jnp.bfloat16),
            pltpu.VMEM((blocks * span, cols), jnp.float32),
        ],
        compiler_params=pltpu.CompilerParams(vmem_limit_bytes=48 * 1024 * 1024),
    )(width, level, parts)


def row_scale(width_f, nlon_all):
    cycle_cols = jnp.arange(nlon_all)
    distance = jnp.minimum(cycle_cols, nlon_all - cycle_cols).astype(jnp.float32)[None, :]
    width_f = width_f[:, None]
    weights_raw = jnp.where(
        distance <= width_f, jnp.exp(-2.0 * distance * distance / (width_f * width_f)), 0.0
    )
    return 1.0 / jnp.sqrt(jnp.sum(weights_raw * weights_raw, axis=1))


def far_halo(near, lat_index, lat_count, lon_count):
    last = X_RUN - 1
    send = jnp.where(lat_index % X_RUN == last, near[-HALF_LAT:], near[:HALF_LAT])

    def across(lat, lon):
        return {last: (lat + 1, lon), 0: (lat - 1, lon)}.get(lat % X_RUN)

    return lax.ppermute(send, ("lat", "lon"), flat_pairs(lat_count, lon_count, across))


def next_halo(along, lat_count, lon_count):
    axes = ("lat", "lon")
    last = X_RUN - 1
    pairs = functools.partial(flat_pairs, lat_count, lon_count)
    low = lax.ppermute(
        along[-HALF_LAT:],
        axes,
        pairs(lambda lat, lon: (lat + 1, lon) if lat % X_RUN != last else None),
    )
    high = lax.ppermute(
        along[:HALF_LAT],
        axes,
        pairs(lambda lat, lon: (lat - 1, lon) if lat % X_RUN != 0 else None),
    )
    return low, high


def body(members, support):
    member_count, lat_rows, lon_cols = members.shape
    lat_count = lax.axis_size("lat")
    lon_count = lax.axis_size("lon")
    nlon_all = lon_count * lon_cols
    nlat_all = lat_count * lat_rows
    lat_index = lax.axis_index("lat")
    axes = ("lat", "lon")

    def polar_of(lat):
        return (lat * lat_rows < POLAR) | ((lat + 1) * lat_rows > nlat_all - POLAR)

    pairs = functools.partial(flat_pairs, lat_count, lon_count)
    data = members.transpose(1, 0, 2)
    lon_index = lax.axis_index("lon")

    shares = len(HELPERS[0])
    share = lat_rows // shares
    helped = {h: (p, q) for p, hs in HELPERS.items() for q, h in enumerate(hs)}
    pieces = lon_count // share
    is_polar = polar_of(lat_index)
    takes_part = functools.reduce(lambda a, b: a | b, [lat_index == i for i in helped])
    keeps = functools.reduce(lambda a, b: a | b, [lat_index == p for p in HELPERS if p in helped])
    row_of = jnp.array(
        [helped[i][0] * lat_rows + helped[i][1] * share if i in helped else 0 for i in range(lat_count)]
    )[lat_index]

    def hands(q):
        return lambda lat, lon: (
            (HELPERS[lat][q], lon) if lat in HELPERS and HELPERS[lat][q] != lat else None
        )

    def returns(q):
        return lambda lat, lon: (
            (helped[lat][0], lon) if lat in helped and helped[lat][1] == q and helped[lat][0] != lat else None
        )

    handed = [
        lax.ppermute(data[q * share : (q + 1) * share], axes, pairs(hands(q))) for q in range(shares)
    ]
    handed[1], late = lax.optimization_barrier((handed[1], data))
    given = jnp.where(keeps, data[:share], sum(handed))
    parts = given.reshape(lon_count, member_count // pieces, lon_cols)

    left = lax.ppermute(
        data, axes, pairs(lambda lat, lon: None if polar_of(lat) else (lat, lon + 1))
    )
    right = lax.ppermute(
        late, axes, pairs(lambda lat, lon: None if polar_of(lat) else (lat, lon - 1))
    )
    widths = lax.dynamic_slice_in_dim(support, lat_index * lat_rows, lat_rows).astype(jnp.float32)
    unit_width = lax.dynamic_slice_in_dim(support, row_of + lon_index // pieces, 1).astype(jnp.float32)
    levels = jnp.log2(row_scale(jnp.concatenate([widths, unit_width]), nlon_all))
    levels, unit_level = levels[:lat_rows], levels[lat_rows:]

    def helping(parts):
        parts = lax.all_to_all(parts, "lon", 0, 0)
        return lax.all_to_all(unit_product(parts, unit_width, unit_level), "lon", 0, 0)

    parts = lax.cond(takes_part, helping, lambda v: v, parts)
    parts, left, right = lax.optimization_barrier((parts, left, right))
    near = near_product(left, data, right, widths, levels)

    far = far_halo(near, lat_index, lat_count, lon_count)
    done = parts.reshape(share, member_count, lon_cols)
    polar = [lax.ppermute(done, axes, pairs(returns(q))) for q in range(shares)]
    polar[0] = jnp.where(keeps, done, polar[0])
    polar = jnp.concatenate(polar, axis=0)
    along = jnp.where(is_polar, polar, near)
    low, high = next_halo(along, lat_count, lon_count)

    half_rows = HALF_LAT
    source_rows = jnp.arange(lat_rows + 2 * half_rows)
    own_rows = jnp.arange(lat_rows)
    offsets_band = (source_rows[:, None] - half_rows - own_rows[None, :]).astype(jnp.float32)
    banded = jnp.where(
        jnp.abs(offsets_band) <= half_rows,
        jnp.exp(-2.0 * offsets_band * offsets_band / (half_rows * half_rows)),
        0.0,
    ).astype(jnp.bfloat16)
    global_rows = lat_index * lat_rows + own_rows
    offsets = jnp.arange(-half_rows, half_rows + 1)
    offset_f = offsets.astype(jnp.float32)
    values = jnp.exp(-2.0 * offset_f * offset_f / (half_rows * half_rows))
    reached = global_rows[:, None] + offsets[None, :]
    inside = (reached >= 0) & (reached < nlat_all)
    lat_norms = 1.0 / jnp.sqrt(jnp.sum(jnp.where(inside, (values * values)[None, :], 0.0), axis=1))
    lower, own, upper = banded[:half_rows], banded[half_rows:-half_rows], banded[-half_rows:]
    x = lat_index % X_RUN
    taps = jnp.where(x == 0, lower, upper)
    first = jnp.einsum(
        "jmc,jr->mrc",
        jnp.concatenate([far, along], axis=0),
        jnp.concatenate([taps, own], axis=0),
        preferred_element_type=jnp.float32,
    )
    first = lax.optimization_barrier(first)
    second = jnp.einsum(
        "jmc,jr->mrc",
        jnp.concatenate([low, high], axis=0),
        jnp.concatenate([lower, upper], axis=0),
        preferred_element_type=jnp.float32,
    )
    return (first + second) * lat_norms[None, :, None]


def solution(mesh):
    placed = (P(None, "lat", "lon"), P())
    return jax.shard_map(
        body, mesh=mesh, in_specs=placed, out_specs=P(None, "lat", "lon"), check_vma=False
    )
```

```python
import functools
import math

import jax
import jax.numpy as jnp
from jax import lax
from jax.experimental import pallas as pl
from jax.experimental.pallas import tpu as pltpu
from jax.sharding import PartitionSpec as P

HALF_LAT = 24
POLAR = 64
X_RUN = 4
HELPERS = {0: (2, 10, 26, 18), 1: (1, 9, 25, 17), 30: (30, 22, 6, 14), 31: (29, 21, 5, 13)}
TILE = 128
LOG2E = math.log2(math.e)


def flat_pairs(lat_count, lon_count, target):
    pairs = []
    for lat in range(lat_count):
        for lon in range(lon_count):
            to = target(lat, lon)
            if to is not None and 0 <= to[0] < lat_count:
                pairs.append((lat * lon_count + lon, to[0] * lon_count + to[1] % lon_count))
    return pairs


def difference(shape):
    return (lax.broadcasted_iota(jnp.int32, shape, 0) - lax.broadcasted_iota(jnp.int32, shape, 1)).astype(jnp.float32)

def toeplitz(distance_sq, square, falloff, level):
    value = jnp.exp2(distance_sq * falloff + level)
    return jnp.where(distance_sq <= square, value, 0.0).astype(jnp.bfloat16)


def near_kernel(width_ref, level_ref, left_ref, mid_ref, right_ref, out_ref):
    rows = mid_ref.shape[0]
    first = pl.program_id(0) * rows
    base = difference((TILE, TILE))
    distances = {k: (base + float(k * TILE)) * (base + float(k * TILE)) for k in range(-2, 3)}
    for row in range(rows):
        width = width_ref[first + row]
        level = level_ref[first + row]
        square = width * width
        falloff = (-2.0 * LOG2E) / square
        t = {}
        for k in range(-2, 3):
            t[k] = toeplitz(distances[k], square, falloff, level)
        weights = jnp.concatenate([t[k] for k in range(-2, 3)], axis=0)
        data = jnp.concatenate([left_ref[row], mid_ref[row], right_ref[row]], axis=1)
        both = jnp.concatenate([data[:, : 5 * TILE], data[:, TILE:]], axis=0)
        got = jnp.dot(both, weights, preferred_element_type=jnp.float32).astype(jnp.bfloat16)
        half = data.shape[0]
        out_ref[row] = jnp.concatenate([got[:half], got[half:]], axis=1)


def near_product(left, mid, right, widths, levels):
    rows, members, cols = mid.shape
    step = 16
    block = pl.BlockSpec((step, members, cols), lambda i: (i, 0, 0))
    smem = pl.BlockSpec(memory_space=pltpu.SMEM)
    return pl.pallas_call(
        near_kernel,
        grid=(rows // step,),
        in_specs=[smem, smem, block, block, block],
        out_specs=block,
        out_shape=jax.ShapeDtypeStruct(mid.shape, jnp.bfloat16),
        compiler_params=pltpu.CompilerParams(vmem_limit_bytes=48 * 1024 * 1024),
    )(widths, levels, left, mid, right)


def circle_kernel(width_ref, level_ref, data_ref, out_ref, tiles, twice, total):
    blocks, members, cols = data_ref.shape
    members, cols = members // 2, cols * 2
    span = twice.shape[0] // (2 * blocks)
    size = blocks * span
    count = blocks * cols // TILE
    base = difference((TILE, TILE))
    width = width_ref[0]
    level = level_ref[0]
    square = width * width
    falloff = (-2.0 * LOG2E) / square
    for n in range(count // 2 + 1):
        distance = jnp.abs(base + float(n * TILE))
        distance = jnp.minimum(distance, float(count * TILE) - distance)
        tile = toeplitz(distance * distance, square, falloff, level)
        tiles[n] = tile
        if 0 < n < count // 2:
            tiles[count - n] = tile.T
    pad = jnp.zeros((span - members, cols), jnp.bfloat16)
    for i in range(blocks):
        halves = data_ref[i]
        block = jnp.concatenate([halves[:members], halves[members:]], axis=1)
        block = jnp.concatenate([block, pad], axis=0)
        twice[i * span : (i + 1) * span] = block
        twice[size + i * span : size + (i + 1) * span] = block
    for k in range(blocks):
        weights = jnp.concatenate(
            [
                jnp.concatenate([tiles[2 * k], tiles[(2 * k - 1) % count]], axis=1),
                jnp.concatenate([tiles[(2 * k + 1) % count], tiles[2 * k]], axis=1),
            ],
            axis=0,
        )
        part = jnp.dot(twice[k * span : k * span + size], weights, preferred_element_type=jnp.float32)
        if k == 0:
            total[...] = part
        else:
            total[...] += part
    for i in range(blocks):
        block = total[i * span : i * span + members].astype(jnp.bfloat16)
        out_ref[i] = jnp.concatenate([block[:, : cols // 2], block[:, cols // 2 :]], axis=0)


def unit_product(parts, width, level):
    blocks, members, cols = parts.shape
    members, cols = members // 2, cols * 2
    span = members + -members % 16
    smem = pl.BlockSpec(memory_space=pltpu.SMEM)
    vmem = pl.BlockSpec(memory_space=pltpu.VMEM)
    return pl.pallas_call(
        circle_kernel,
        in_specs=[smem, smem, vmem],
        out_specs=vmem,
        out_shape=jax.ShapeDtypeStruct(parts.shape, jnp.bfloat16),
        scratch_shapes=[
            pltpu.VMEM((blocks * cols // TILE, TILE, TILE), jnp.bfloat16),
            pltpu.VMEM((2 * blocks * span, cols), jnp.bfloat16),
            pltpu.VMEM((blocks * span, cols), jnp.float32),
        ],
        compiler_params=pltpu.CompilerParams(vmem_limit_bytes=48 * 1024 * 1024),
    )(width, level, parts)


def row_scale(width_f, nlon_all):
    cycle_cols = jnp.arange(nlon_all)
    distance = jnp.minimum(cycle_cols, nlon_all - cycle_cols).astype(jnp.float32)[None, :]
    width_f = width_f[:, None]
    weights_raw = jnp.where(
        distance <= width_f, jnp.exp(-2.0 * distance * distance / (width_f * width_f)), 0.0
    )
    return 1.0 / jnp.sqrt(jnp.sum(weights_raw * weights_raw, axis=1))


def far_halo(near, lat_index, lat_count, lon_count):
    last = X_RUN - 1
    send = jnp.where(lat_index % X_RUN == last, near[-HALF_LAT:], near[:HALF_LAT])

    def across(lat, lon):
        return {last: (lat + 1, lon), 0: (lat - 1, lon)}.get(lat % X_RUN)

    return lax.ppermute(send, ("lat", "lon"), flat_pairs(lat_count, lon_count, across))


def next_halo(along, lat_count, lon_count):
    axes = ("lat", "lon")
    last = X_RUN - 1
    pairs = functools.partial(flat_pairs, lat_count, lon_count)
    low = lax.ppermute(
        along[-HALF_LAT:],
        axes,
        pairs(lambda lat, lon: (lat + 1, lon) if lat % X_RUN != last else None),
    )
    high = lax.ppermute(
        along[:HALF_LAT],
        axes,
        pairs(lambda lat, lon: (lat - 1, lon) if lat % X_RUN != 0 else None),
    )
    return low, high


def body(members, support):
    member_count, lat_rows, lon_cols = members.shape
    lat_count = lax.axis_size("lat")
    lon_count = lax.axis_size("lon")
    nlon_all = lon_count * lon_cols
    nlat_all = lat_count * lat_rows
    lat_index = lax.axis_index("lat")
    axes = ("lat", "lon")

    def polar_of(lat):
        return (lat * lat_rows < POLAR) | ((lat + 1) * lat_rows > nlat_all - POLAR)

    pairs = functools.partial(flat_pairs, lat_count, lon_count)
    data = members.transpose(1, 0, 2)
    lon_index = lax.axis_index("lon")

    shares = len(HELPERS[0])
    share = lat_rows // shares
    helped = {h: (p, q) for p, hs in HELPERS.items() for q, h in enumerate(hs)}
    pieces = lon_count // share
    is_polar = polar_of(lat_index)
    takes_part = functools.reduce(lambda a, b: a | b, [lat_index == i for i in helped])
    keeps = functools.reduce(lambda a, b: a | b, [lat_index == p for p in HELPERS if p in helped])
    row_of = jnp.array(
        [helped[i][0] * lat_rows + helped[i][1] * share if i in helped else 0 for i in range(lat_count)]
    )[lat_index]

    def hands(q):
        return lambda lat, lon: (
            (HELPERS[lat][q], lon) if lat in HELPERS and HELPERS[lat][q] != lat else None
        )

    def returns(q):
        return lambda lat, lon: (
            (helped[lat][0], lon) if lat in helped and helped[lat][1] == q and helped[lat][0] != lat else None
        )

    handed = [
        lax.ppermute(data[q * share : (q + 1) * share], axes, pairs(hands(q))) for q in range(shares)
    ]
    handed[1], late = lax.optimization_barrier((handed[1], data))
    given = jnp.where(keeps, data[:share], sum(handed))
    group = member_count // pieces
    parts = given.reshape(share, pieces, group, 2, lon_cols // 2).transpose(0, 1, 3, 2, 4)
    parts = parts.reshape(lon_count, 2 * group, lon_cols // 2)

    left = lax.ppermute(
        data, axes, pairs(lambda lat, lon: None if polar_of(lat) else (lat, lon + 1))
    )
    right = lax.ppermute(
        late, axes, pairs(lambda lat, lon: None if polar_of(lat) else (lat, lon - 1))
    )
    widths = lax.dynamic_slice_in_dim(support, lat_index * lat_rows, lat_rows).astype(jnp.float32)
    unit_width = lax.dynamic_slice_in_dim(support, row_of + lon_index // pieces, 1).astype(jnp.float32)
    levels = jnp.log2(row_scale(jnp.concatenate([widths, unit_width]), nlon_all))
    levels, unit_level = levels[:lat_rows], levels[lat_rows:]

    def helping(parts):
        parts = lax.all_to_all(parts, "lon", 0, 0)
        return lax.all_to_all(unit_product(parts, unit_width, unit_level), "lon", 0, 0)

    parts = lax.cond(takes_part, helping, lambda v: v, parts)
    parts, left, right = lax.optimization_barrier((parts, left, right))
    near = near_product(left, data, right, widths, levels)

    far = far_halo(near, lat_index, lat_count, lon_count)
    done = parts.reshape(share, pieces, 2, group, lon_cols // 2).transpose(0, 1, 3, 2, 4)
    done = done.reshape(share, member_count, lon_cols)
    polar = [lax.ppermute(done, axes, pairs(returns(q))) for q in range(shares)]
    polar[0] = jnp.where(keeps, done, polar[0])
    polar = jnp.concatenate(polar, axis=0)
    along = jnp.where(is_polar, polar, near)
    low, high = next_halo(along, lat_count, lon_count)

    half_rows = HALF_LAT
    source_rows = jnp.arange(lat_rows + 2 * half_rows)
    own_rows = jnp.arange(lat_rows)
    offsets_band = (source_rows[:, None] - half_rows - own_rows[None, :]).astype(jnp.float32)
    banded = jnp.where(
        jnp.abs(offsets_band) <= half_rows,
        jnp.exp(-2.0 * offsets_band * offsets_band / (half_rows * half_rows)),
        0.0,
    ).astype(jnp.bfloat16)
    global_rows = lat_index * lat_rows + own_rows
    offsets = jnp.arange(-half_rows, half_rows + 1)
    offset_f = offsets.astype(jnp.float32)
    values = jnp.exp(-2.0 * offset_f * offset_f / (half_rows * half_rows))
    reached = global_rows[:, None] + offsets[None, :]
    inside = (reached >= 0) & (reached < nlat_all)
    lat_norms = 1.0 / jnp.sqrt(jnp.sum(jnp.where(inside, (values * values)[None, :], 0.0), axis=1))
    lower, own, upper = banded[:half_rows], banded[half_rows:-half_rows], banded[-half_rows:]
    x = lat_index % X_RUN
    taps = jnp.where(x == 0, lower, upper)
    first = jnp.einsum(
        "jmc,jr->mrc",
        jnp.concatenate([far, along], axis=0),
        jnp.concatenate([taps, own], axis=0),
        preferred_element_type=jnp.float32,
    )
    first = lax.optimization_barrier(first)
    second = jnp.einsum(
        "jmc,jr->mrc",
        jnp.concatenate([low, high], axis=0),
        jnp.concatenate([lower, upper], axis=0),
        preferred_element_type=jnp.float32,
    )
    return (first + second) * lat_norms[None, :, None]


def solution(mesh):
    placed = (P(None, "lat", "lon"), P())
    return jax.shard_map(
        body, mesh=mesh, in_specs=placed, out_specs=P(None, "lat", "lon"), check_vma=False
    )
```

```python
import functools
import math

import jax
import jax.numpy as jnp
from jax import lax
from jax.experimental import pallas as pl
from jax.experimental.pallas import tpu as pltpu
from jax.sharding import PartitionSpec as P

HALF_LAT = 24
POLAR = 64
X_RUN = 4
HELPERS = {0: (2, 10, 26, 18), 1: (1, 9, 25, 17), 30: (30, 22, 6, 14), 31: (29, 21, 5, 13)}
TILE = 128
LOG2E = math.log2(math.e)


def flat_pairs(lat_count, lon_count, target):
    pairs = []
    for lat in range(lat_count):
        for lon in range(lon_count):
            to = target(lat, lon)
            if to is not None and 0 <= to[0] < lat_count:
                pairs.append((lat * lon_count + lon, to[0] * lon_count + to[1] % lon_count))
    return pairs


def difference(shape):
    return (lax.broadcasted_iota(jnp.int32, shape, 0) - lax.broadcasted_iota(jnp.int32, shape, 1)).astype(jnp.float32)

def toeplitz(distance_sq, square, falloff, level):
    value = jnp.exp2(distance_sq * falloff + level)
    return jnp.where(distance_sq <= square, value, 0.0).astype(jnp.bfloat16)


def near_kernel(width_ref, level_ref, left_ref, mid_ref, right_ref, out_ref):
    rows = mid_ref.shape[0]
    first = pl.program_id(0) * rows
    base = difference((TILE, TILE))
    distances = {k: (base + float(k * TILE)) * (base + float(k * TILE)) for k in range(-2, 3)}
    for row in range(rows):
        width = width_ref[first + row]
        level = level_ref[first + row]
        square = width * width
        falloff = (-2.0 * LOG2E) / square
        t = {}
        for k in range(-2, 3):
            t[k] = toeplitz(distances[k], square, falloff, level)
        weights = jnp.concatenate([t[k] for k in range(-2, 3)], axis=0)
        data = jnp.concatenate([left_ref[row], mid_ref[row], right_ref[row]], axis=1)
        both = jnp.concatenate([data[:, : 5 * TILE], data[:, TILE:]], axis=0)
        got = jnp.dot(both, weights, preferred_element_type=jnp.float32).astype(jnp.bfloat16)
        half = data.shape[0]
        out_ref[row] = jnp.concatenate([got[:half], got[half:]], axis=1)


def near_product(left, mid, right, widths, levels):
    rows, members, cols = mid.shape
    step = 16
    block = pl.BlockSpec((step, members, cols), lambda i: (i, 0, 0))
    smem = pl.BlockSpec(memory_space=pltpu.SMEM)
    return pl.pallas_call(
        near_kernel,
        grid=(rows // step,),
        in_specs=[smem, smem, block, block, block],
        out_specs=block,
        out_shape=jax.ShapeDtypeStruct(mid.shape, jnp.bfloat16),
        compiler_params=pltpu.CompilerParams(vmem_limit_bytes=48 * 1024 * 1024),
    )(widths, levels, left, mid, right)


def circle_kernel(width_ref, level_ref, data_ref, out_ref, tiles, twice, total):
    blocks, members, cols = data_ref.shape
    members, cols = members // 2, cols * 2
    span = twice.shape[0] // (2 * blocks)
    size = blocks * span
    count = blocks * cols // TILE
    base = difference((TILE, TILE))
    width = width_ref[0]
    level = level_ref[0]
    square = width * width
    falloff = (-2.0 * LOG2E) / square
    for n in range(count // 2 + 1):
        distance = jnp.abs(base + float(n * TILE))
        distance = jnp.minimum(distance, float(count * TILE) - distance)
        tile = toeplitz(distance * distance, square, falloff, level)
        tiles[n] = tile
        if 0 < n < count // 2:
            tiles[count - n] = tile.T
    pad = jnp.zeros((span - members, cols), jnp.bfloat16)
    for i in range(blocks):
        halves = data_ref[i]
        block = jnp.concatenate([halves[:members], halves[members:]], axis=1)
        block = jnp.concatenate([block, pad], axis=0)
        twice[i * span : (i + 1) * span] = block
        twice[size + i * span : size + (i + 1) * span] = block
    step = 4
    for first in range(0, blocks, step):
        steps = range(first, first + step)
        weights = [
            jnp.concatenate([tiles[(2 * k + half) % count], tiles[(2 * k + half - 1) % count]], axis=1)
            for k in steps
            for half in range(2)
        ]
        data = jnp.concatenate([twice[k * span : k * span + size] for k in steps], axis=1)
        part = jnp.dot(data, jnp.concatenate(weights, axis=0), preferred_element_type=jnp.float32)
        if first == 0:
            total[...] = part
        else:
            total[...] += part
    for i in range(blocks):
        block = total[i * span : i * span + members].astype(jnp.bfloat16)
        out_ref[i] = jnp.concatenate([block[:, : cols // 2], block[:, cols // 2 :]], axis=0)


def unit_product(parts, width, level):
    blocks, members, cols = parts.shape
    members, cols = members // 2, cols * 2
    span = members + -members % 16
    smem = pl.BlockSpec(memory_space=pltpu.SMEM)
    vmem = pl.BlockSpec(memory_space=pltpu.VMEM)
    return pl.pallas_call(
        circle_kernel,
        in_specs=[smem, smem, vmem],
        out_specs=vmem,
        out_shape=jax.ShapeDtypeStruct(parts.shape, jnp.bfloat16),
        scratch_shapes=[
            pltpu.VMEM((blocks * cols // TILE, TILE, TILE), jnp.bfloat16),
            pltpu.VMEM((2 * blocks * span, cols), jnp.bfloat16),
            pltpu.VMEM((blocks * span, cols), jnp.float32),
        ],
        compiler_params=pltpu.CompilerParams(vmem_limit_bytes=48 * 1024 * 1024),
    )(width, level, parts)


def row_scale(width_f, nlon_all):
    cycle_cols = jnp.arange(nlon_all)
    distance = jnp.minimum(cycle_cols, nlon_all - cycle_cols).astype(jnp.float32)[None, :]
    width_f = width_f[:, None]
    weights_raw = jnp.where(
        distance <= width_f, jnp.exp(-2.0 * distance * distance / (width_f * width_f)), 0.0
    )
    return 1.0 / jnp.sqrt(jnp.sum(weights_raw * weights_raw, axis=1))


def far_halo(near, lat_index, lat_count, lon_count):
    last = X_RUN - 1
    send = jnp.where(lat_index % X_RUN == last, near[-HALF_LAT:], near[:HALF_LAT])

    def across(lat, lon):
        return {last: (lat + 1, lon), 0: (lat - 1, lon)}.get(lat % X_RUN)

    return lax.ppermute(send, ("lat", "lon"), flat_pairs(lat_count, lon_count, across))


def next_halo(along, lat_count, lon_count):
    axes = ("lat", "lon")
    last = X_RUN - 1
    pairs = functools.partial(flat_pairs, lat_count, lon_count)
    low = lax.ppermute(
        along[-HALF_LAT:],
        axes,
        pairs(lambda lat, lon: (lat + 1, lon) if lat % X_RUN != last else None),
    )
    high = lax.ppermute(
        along[:HALF_LAT],
        axes,
        pairs(lambda lat, lon: (lat - 1, lon) if lat % X_RUN != 0 else None),
    )
    return low, high


def body(members, support):
    member_count, lat_rows, lon_cols = members.shape
    lat_count = lax.axis_size("lat")
    lon_count = lax.axis_size("lon")
    nlon_all = lon_count * lon_cols
    nlat_all = lat_count * lat_rows
    lat_index = lax.axis_index("lat")
    axes = ("lat", "lon")

    def polar_of(lat):
        return (lat * lat_rows < POLAR) | ((lat + 1) * lat_rows > nlat_all - POLAR)

    pairs = functools.partial(flat_pairs, lat_count, lon_count)
    data = members.transpose(1, 0, 2)
    lon_index = lax.axis_index("lon")

    shares = len(HELPERS[0])
    share = lat_rows // shares
    helped = {h: (p, q) for p, hs in HELPERS.items() for q, h in enumerate(hs)}
    pieces = lon_count // share
    is_polar = polar_of(lat_index)
    takes_part = functools.reduce(lambda a, b: a | b, [lat_index == i for i in helped])
    keeps = functools.reduce(lambda a, b: a | b, [lat_index == p for p in HELPERS if p in helped])
    row_of = jnp.array(
        [helped[i][0] * lat_rows + helped[i][1] * share if i in helped else 0 for i in range(lat_count)]
    )[lat_index]

    def hands(q):
        return lambda lat, lon: (
            (HELPERS[lat][q], lon) if lat in HELPERS and HELPERS[lat][q] != lat else None
        )

    def returns(q):
        return lambda lat, lon: (
            (helped[lat][0], lon) if lat in helped and helped[lat][1] == q and helped[lat][0] != lat else None
        )

    handed = [
        lax.ppermute(data[q * share : (q + 1) * share], axes, pairs(hands(q))) for q in range(shares)
    ]
    handed[1], late = lax.optimization_barrier((handed[1], data))
    given = jnp.where(keeps, data[:share], sum(handed))
    group = member_count // pieces
    parts = given.reshape(share, pieces, group, 2, lon_cols // 2).transpose(0, 1, 3, 2, 4)
    parts = parts.reshape(lon_count, 2 * group, lon_cols // 2)

    left = lax.ppermute(
        data, axes, pairs(lambda lat, lon: None if polar_of(lat) else (lat, lon + 1))
    )
    right = lax.ppermute(
        late, axes, pairs(lambda lat, lon: None if polar_of(lat) else (lat, lon - 1))
    )
    widths = lax.dynamic_slice_in_dim(support, lat_index * lat_rows, lat_rows).astype(jnp.float32)
    unit_width = lax.dynamic_slice_in_dim(support, row_of + lon_index // pieces, 1).astype(jnp.float32)
    levels = jnp.log2(row_scale(jnp.concatenate([widths, unit_width]), nlon_all))
    levels, unit_level = levels[:lat_rows], levels[lat_rows:]

    def helping(parts):
        parts = lax.all_to_all(parts, "lon", 0, 0)
        return lax.all_to_all(unit_product(parts, unit_width, unit_level), "lon", 0, 0)

    parts = lax.cond(takes_part, helping, lambda v: v, parts)
    parts, left, right = lax.optimization_barrier((parts, left, right))
    near = near_product(left, data, right, widths, levels)

    far = far_halo(near, lat_index, lat_count, lon_count)
    done = parts.reshape(share, pieces, 2, group, lon_cols // 2).transpose(0, 1, 3, 2, 4)
    done = done.reshape(share, member_count, lon_cols)
    polar = [lax.ppermute(done, axes, pairs(returns(q))) for q in range(shares)]
    polar[0] = jnp.where(keeps, done, polar[0])
    polar = jnp.concatenate(polar, axis=0)
    along = jnp.where(is_polar, polar, near)
    low, high = next_halo(along, lat_count, lon_count)

    half_rows = HALF_LAT
    source_rows = jnp.arange(lat_rows + 2 * half_rows)
    own_rows = jnp.arange(lat_rows)
    offsets_band = (source_rows[:, None] - half_rows - own_rows[None, :]).astype(jnp.float32)
    banded = jnp.where(
        jnp.abs(offsets_band) <= half_rows,
        jnp.exp(-2.0 * offsets_band * offsets_band / (half_rows * half_rows)),
        0.0,
    ).astype(jnp.bfloat16)
    global_rows = lat_index * lat_rows + own_rows
    offsets = jnp.arange(-half_rows, half_rows + 1)
    offset_f = offsets.astype(jnp.float32)
    values = jnp.exp(-2.0 * offset_f * offset_f / (half_rows * half_rows))
    reached = global_rows[:, None] + offsets[None, :]
    inside = (reached >= 0) & (reached < nlat_all)
    lat_norms = 1.0 / jnp.sqrt(jnp.sum(jnp.where(inside, (values * values)[None, :], 0.0), axis=1))
    lower, own, upper = banded[:half_rows], banded[half_rows:-half_rows], banded[-half_rows:]
    x = lat_index % X_RUN
    taps = jnp.where(x == 0, lower, upper)
    first = jnp.einsum(
        "jmc,jr->mrc",
        jnp.concatenate([far, along], axis=0),
        jnp.concatenate([taps, own], axis=0),
        preferred_element_type=jnp.float32,
    )
    first = lax.optimization_barrier(first)
    second = jnp.einsum(
        "jmc,jr->mrc",
        jnp.concatenate([low, high], axis=0),
        jnp.concatenate([lower, upper], axis=0),
        preferred_element_type=jnp.float32,
    )
    return (first + second) * lat_norms[None, :, None]


def solution(mesh):
    placed = (P(None, "lat", "lon"), P())
    return jax.shard_map(
        body, mesh=mesh, in_specs=placed, out_specs=P(None, "lat", "lon"), check_vma=False
    )
```

```python
import functools
import math

import jax
import jax.numpy as jnp
from jax import lax
from jax.experimental import pallas as pl
from jax.experimental.pallas import tpu as pltpu
from jax.sharding import PartitionSpec as P

HALF_LAT = 24
POLAR = 64
X_RUN = 4
HELPERS = {0: (2, 10, 26, 18), 1: (1, 9, 25, 17), 30: (30, 22, 6, 14), 31: (29, 21, 5, 13)}
TILE = 128
LOG2E = math.log2(math.e)


def flat_pairs(lat_count, lon_count, target):
    pairs = []
    for lat in range(lat_count):
        for lon in range(lon_count):
            to = target(lat, lon)
            if to is not None and 0 <= to[0] < lat_count:
                pairs.append((lat * lon_count + lon, to[0] * lon_count + to[1] % lon_count))
    return pairs


def difference(shape):
    return (lax.broadcasted_iota(jnp.int32, shape, 0) - lax.broadcasted_iota(jnp.int32, shape, 1)).astype(jnp.float32)

def toeplitz(distance_sq, square, falloff, level):
    value = jnp.exp2(distance_sq * falloff + level)
    return jnp.where(distance_sq <= square, value, 0.0).astype(jnp.bfloat16)


def near_kernel(width_ref, level_ref, left_ref, mid_ref, right_ref, out_ref):
    rows = mid_ref.shape[0]
    first = pl.program_id(0) * rows
    base = difference((TILE, TILE))
    distances = {k: (base + float(k * TILE)) * (base + float(k * TILE)) for k in range(-2, 3)}
    for row in range(rows):
        width = width_ref[first + row]
        level = level_ref[first + row]
        square = width * width
        falloff = (-2.0 * LOG2E) / square
        t = {}
        for k in range(-2, 3):
            t[k] = toeplitz(distances[k], square, falloff, level)
        weights = jnp.concatenate([t[k] for k in range(-2, 3)], axis=0)
        data = jnp.concatenate([left_ref[row], mid_ref[row], right_ref[row]], axis=1)
        both = jnp.concatenate([data[:, : 5 * TILE], data[:, TILE:]], axis=0)
        got = jnp.dot(both, weights, preferred_element_type=jnp.float32).astype(jnp.bfloat16)
        half = data.shape[0]
        out_ref[row] = jnp.concatenate([got[:half], got[half:]], axis=1)


def near_product(left, mid, right, widths, levels):
    rows, members, cols = mid.shape
    step = rows
    block = pl.BlockSpec((step, members, cols), lambda i: (i, 0, 0))
    smem = pl.BlockSpec(memory_space=pltpu.SMEM)
    return pl.pallas_call(
        near_kernel,
        grid=(rows // step,),
        in_specs=[smem, smem, block, block, block],
        out_specs=block,
        out_shape=jax.ShapeDtypeStruct(mid.shape, jnp.bfloat16),
        compiler_params=pltpu.CompilerParams(vmem_limit_bytes=48 * 1024 * 1024),
    )(widths, levels, left, mid, right)


def circle_kernel(width_ref, level_ref, data_ref, out_ref, tiles, twice, total):
    blocks, members, cols = data_ref.shape
    members, cols = members // 2, cols * 2
    span = twice.shape[0] // (2 * blocks)
    size = blocks * span
    count = blocks * cols // TILE
    base = difference((TILE, TILE))
    width = width_ref[0]
    level = level_ref[0]
    square = width * width
    falloff = (-2.0 * LOG2E) / square
    for n in range(count // 2 + 1):
        distance = jnp.abs(base + float(n * TILE))
        distance = jnp.minimum(distance, float(count * TILE) - distance)
        tile = toeplitz(distance * distance, square, falloff, level)
        tiles[n] = tile
        if 0 < n < count // 2:
            tiles[count - n] = tile.T
    pad = jnp.zeros((span - members, cols), jnp.bfloat16)
    for i in range(blocks):
        halves = data_ref[i]
        block = jnp.concatenate([halves[:members], halves[members:]], axis=1)
        block = jnp.concatenate([block, pad], axis=0)
        twice[i * span : (i + 1) * span] = block
        twice[size + i * span : size + (i + 1) * span] = block
    step = 4
    for first in range(0, blocks, step):
        steps = range(first, first + step)
        weights = [
            jnp.concatenate([tiles[(2 * k + half) % count], tiles[(2 * k + half - 1) % count]], axis=1)
            for k in steps
            for half in range(2)
        ]
        data = jnp.concatenate([twice[k * span : k * span + size] for k in steps], axis=1)
        part = jnp.dot(data, jnp.concatenate(weights, axis=0), preferred_element_type=jnp.float32)
        if first == 0:
            total[...] = part
        else:
            total[...] += part
    for i in range(blocks):
        block = total[i * span : i * span + members].astype(jnp.bfloat16)
        out_ref[i] = jnp.concatenate([block[:, : cols // 2], block[:, cols // 2 :]], axis=0)


def unit_product(parts, width, level):
    blocks, members, cols = parts.shape
    members, cols = members // 2, cols * 2
    span = members + -members % 16
    smem = pl.BlockSpec(memory_space=pltpu.SMEM)
    vmem = pl.BlockSpec(memory_space=pltpu.VMEM)
    return pl.pallas_call(
        circle_kernel,
        in_specs=[smem, smem, vmem],
        out_specs=vmem,
        out_shape=jax.ShapeDtypeStruct(parts.shape, jnp.bfloat16),
        scratch_shapes=[
            pltpu.VMEM((blocks * cols // TILE, TILE, TILE), jnp.bfloat16),
            pltpu.VMEM((2 * blocks * span, cols), jnp.bfloat16),
            pltpu.VMEM((blocks * span, cols), jnp.float32),
        ],
        compiler_params=pltpu.CompilerParams(vmem_limit_bytes=48 * 1024 * 1024),
    )(width, level, parts)


def row_scale(width_f, nlon_all):
    cycle_cols = jnp.arange(nlon_all)
    distance = jnp.minimum(cycle_cols, nlon_all - cycle_cols).astype(jnp.float32)[None, :]
    width_f = width_f[:, None]
    weights_raw = jnp.where(
        distance <= width_f, jnp.exp(-2.0 * distance * distance / (width_f * width_f)), 0.0
    )
    return 1.0 / jnp.sqrt(jnp.sum(weights_raw * weights_raw, axis=1))


def far_halo(near, lat_index, lat_count, lon_count):
    last = X_RUN - 1
    send = jnp.where(lat_index % X_RUN == last, near[-HALF_LAT:], near[:HALF_LAT])

    def across(lat, lon):
        return {last: (lat + 1, lon), 0: (lat - 1, lon)}.get(lat % X_RUN)

    return lax.ppermute(send, ("lat", "lon"), flat_pairs(lat_count, lon_count, across))


def next_halo(along, lat_count, lon_count):
    axes = ("lat", "lon")
    last = X_RUN - 1
    pairs = functools.partial(flat_pairs, lat_count, lon_count)
    low = lax.ppermute(
        along[-HALF_LAT:],
        axes,
        pairs(lambda lat, lon: (lat + 1, lon) if lat % X_RUN != last else None),
    )
    high = lax.ppermute(
        along[:HALF_LAT],
        axes,
        pairs(lambda lat, lon: (lat - 1, lon) if lat % X_RUN != 0 else None),
    )
    return low, high


def body(members, support):
    member_count, lat_rows, lon_cols = members.shape
    lat_count = lax.axis_size("lat")
    lon_count = lax.axis_size("lon")
    nlon_all = lon_count * lon_cols
    nlat_all = lat_count * lat_rows
    lat_index = lax.axis_index("lat")
    axes = ("lat", "lon")

    def polar_of(lat):
        return (lat * lat_rows < POLAR) | ((lat + 1) * lat_rows > nlat_all - POLAR)

    pairs = functools.partial(flat_pairs, lat_count, lon_count)
    data = members.transpose(1, 0, 2)
    lon_index = lax.axis_index("lon")

    shares = len(HELPERS[0])
    share = lat_rows // shares
    helped = {h: (p, q) for p, hs in HELPERS.items() for q, h in enumerate(hs)}
    pieces = lon_count // share
    is_polar = polar_of(lat_index)
    takes_part = functools.reduce(lambda a, b: a | b, [lat_index == i for i in helped])
    keeps = functools.reduce(lambda a, b: a | b, [lat_index == p for p in HELPERS if p in helped])
    row_of = jnp.array(
        [helped[i][0] * lat_rows + helped[i][1] * share if i in helped else 0 for i in range(lat_count)]
    )[lat_index]

    def hands(q):
        return lambda lat, lon: (
            (HELPERS[lat][q], lon) if lat in HELPERS and HELPERS[lat][q] != lat else None
        )

    def returns(q):
        return lambda lat, lon: (
            (helped[lat][0], lon) if lat in helped and helped[lat][1] == q and helped[lat][0] != lat else None
        )

    handed = [
        lax.ppermute(data[q * share : (q + 1) * share], axes, pairs(hands(q))) for q in range(shares)
    ]
    handed[1], late = lax.optimization_barrier((handed[1], data))
    given = jnp.where(keeps, data[:share], sum(handed))
    group = member_count // pieces
    parts = given.reshape(share, pieces, group, 2, lon_cols // 2).transpose(0, 1, 3, 2, 4)
    parts = parts.reshape(lon_count, 2 * group, lon_cols // 2)

    left = lax.ppermute(
        data, axes, pairs(lambda lat, lon: None if polar_of(lat) else (lat, lon + 1))
    )
    right = lax.ppermute(
        late, axes, pairs(lambda lat, lon: None if polar_of(lat) else (lat, lon - 1))
    )
    widths = lax.dynamic_slice_in_dim(support, lat_index * lat_rows, lat_rows).astype(jnp.float32)
    unit_width = lax.dynamic_slice_in_dim(support, row_of + lon_index // pieces, 1).astype(jnp.float32)
    levels = jnp.log2(row_scale(jnp.concatenate([widths, unit_width]), nlon_all))
    levels, unit_level = levels[:lat_rows], levels[lat_rows:]

    def helping(parts):
        parts = lax.all_to_all(parts, "lon", 0, 0)
        return lax.all_to_all(unit_product(parts, unit_width, unit_level), "lon", 0, 0)

    parts = lax.cond(takes_part, helping, lambda v: v, parts)
    parts, left, right = lax.optimization_barrier((parts, left, right))
    near = near_product(left, data, right, widths, levels)

    far = far_halo(near, lat_index, lat_count, lon_count)
    done = parts.reshape(share, pieces, 2, group, lon_cols // 2).transpose(0, 1, 3, 2, 4)
    done = done.reshape(share, member_count, lon_cols)
    polar = [lax.ppermute(done, axes, pairs(returns(q))) for q in range(shares)]
    polar[0] = jnp.where(keeps, done, polar[0])
    polar = jnp.concatenate(polar, axis=0)
    along = jnp.where(is_polar, polar, near)
    low, high = next_halo(along, lat_count, lon_count)

    half_rows = HALF_LAT
    source_rows = jnp.arange(lat_rows + 2 * half_rows)
    own_rows = jnp.arange(lat_rows)
    offsets_band = (source_rows[:, None] - half_rows - own_rows[None, :]).astype(jnp.float32)
    banded = jnp.where(
        jnp.abs(offsets_band) <= half_rows,
        jnp.exp(-2.0 * offsets_band * offsets_band / (half_rows * half_rows)),
        0.0,
    ).astype(jnp.bfloat16)
    global_rows = lat_index * lat_rows + own_rows
    offsets = jnp.arange(-half_rows, half_rows + 1)
    offset_f = offsets.astype(jnp.float32)
    values = jnp.exp(-2.0 * offset_f * offset_f / (half_rows * half_rows))
    reached = global_rows[:, None] + offsets[None, :]
    inside = (reached >= 0) & (reached < nlat_all)
    lat_norms = 1.0 / jnp.sqrt(jnp.sum(jnp.where(inside, (values * values)[None, :], 0.0), axis=1))
    lower, own, upper = banded[:half_rows], banded[half_rows:-half_rows], banded[-half_rows:]
    x = lat_index % X_RUN
    taps = jnp.where(x == 0, lower, upper)
    first = jnp.einsum(
        "jmc,jr->mrc",
        jnp.concatenate([far, along], axis=0),
        jnp.concatenate([taps, own], axis=0),
        preferred_element_type=jnp.float32,
    )
    first = lax.optimization_barrier(first)
    second = jnp.einsum(
        "jmc,jr->mrc",
        jnp.concatenate([low, high], axis=0),
        jnp.concatenate([lower, upper], axis=0),
        preferred_element_type=jnp.float32,
    )
    return (first + second) * lat_norms[None, :, None]


def solution(mesh):
    placed = (P(None, "lat", "lon"), P())
    return jax.shard_map(
        body, mesh=mesh, in_specs=placed, out_specs=P(None, "lat", "lon"), check_vma=False
    )
```
